32 devices in a mesh: segment: 4 (over x, core), dp: 8 (over z, y).
Axes of the slice: x: 2, y: 2, z: 4, core: 2. Of those that a mesh axis runs over, the one named last changes fastest.
Arguments:
- latents: bfloat16 [2, 1024, 1280], P(None, 'dp'), may hold values from -6 to 6
- cotangent: bfloat16 [2, 1024, 1280], P(None, 'dp'), may hold values from -6 to 6
- timesteps: int32 [2, 8], P(None, 'dp'), may hold values from 0 to 999
- time_table: bfloat16 [4, 1000, 1280], P('segment'), may hold values from -3 to 3
- w_in: bfloat16 [4, 1280, 1280], P('segment'), may hold values from -0.15625 to 0.15625
- w_out: bfloat16 [4, 1280, 1280], P('segment'), may hold values from -0.15625 to 0.15625
- w_skip: bfloat16 [4, 1280, 1280], P('segment'), may hold values from -0.15625 to 0.15625
Outputs:
- phase_out: bfloat16 [4, 2, 1024, 1280], P('segment', None, 'dp')
- input_grads: bfloat16 [4, 2, 1024, 1280], P('segment', None, 'dp')
- grad_w_in: float32 [4, 1280, 1280], P('segment', 'dp')
- grad_w_out: float32 [4, 1280, 1280], P('segment', 'dp')
- grad_w_skip: float32 [4, 1280, 1280], P('segment', 'dp')
The draws below stay inside these ranges and needn't reach their ends.
All inputs are finite; a program needn't handle non-finite values.
Results may differ from the reference program's by a relative error of at most 0.028.
Values may be sent and summed in bfloat16 or wider, within the bound.
No kernel may reach another device: no remote copies, remote signals or barrier semaphores. Data moves between devices by JAX's collectives and lax.ppermute only.
A program may use at most 128 MiB of HBM per device.

```python
import jax
import jax.numpy as jnp

C = 1280
TSTEPS = 1000
MICRO = 2
ROWS = 128
SEGMENTS = 4
SAMPLES = 8
ROWS_ALL = 1024


def with_ends(array, stream_key, least, high):
    longest = array.shape.index(max(array.shape))
    spots = []
    for shift in (0, 1):
        where = [jax.random.randint(jax.random.fold_in(stream_key, axis), (), 0, length) for axis, length in enumerate(array.shape)]
        where[longest] = (where[longest] + shift) % array.shape[longest]
        spots.append(tuple(where))
    return array.at[spots[0]].set(least).at[spots[1]].set(high)


def block_scale(key, dims, pieces, low, top_value):
    loudness = 1.0
    for position, parts in pieces:
        draws = jax.random.uniform(jax.random.fold_in(jax.random.fold_in(key, 6), position), (parts,), jnp.float32, low / len(pieces), top_value / len(pieces))
        loudness = loudness * jnp.repeat(jnp.exp(draws), dims[position] // parts).reshape((-1,) + (1,) * (len(dims) - 1 - position))
    return loudness


def scatter_about(stream_key, extent, scale, limit, pieces=(), dtype=jnp.bfloat16):
    entries = scale * jax.random.normal(stream_key, extent, jnp.float32)
    if pieces:
        entries = entries * block_scale(stream_key, extent, pieces, -0.22, 0.18)
    return jnp.clip(entries, -limit, limit).astype(dtype)


def setup_inputs(seed: int = 0) -> dict:
    splits = jax.random.split(jax.random.key(seed), 8)
    latents = scatter_about(splits[0], (MICRO, ROWS_ALL, C), 1.0, 6.0, ((1, 8),))
    cotangent = scatter_about(splits[1], (MICRO, ROWS_ALL, C), 1.0, 6.0, ((1, 8),))
    timesteps = with_ends(jax.random.randint(splits[2], (MICRO, SAMPLES), 0, TSTEPS), jax.random.fold_in(splits[2], 1), 0, TSTEPS - 1).astype(jnp.int32)
    time_table = scatter_about(splits[3], (SEGMENTS, TSTEPS, C), 0.5, 3.0, ((0, 4),))
    w_in = scatter_about(splits[4], (SEGMENTS, C, C), C ** -0.5, 0.15625, ((0, 4),))
    w_out = scatter_about(splits[5], (SEGMENTS, C, C), C ** -0.5, 0.15625, ((0, 4),))
    w_skip = scatter_about(splits[6], (SEGMENTS, C, C), C ** -0.5, 0.15625, ((0, 4),))
    return dict(latents=latents, cotangent=cotangent, timesteps=timesteps, time_table=time_table, w_in=w_in, w_out=w_out, w_skip=w_skip)


def silu_grad(pre):
    sig = jax.nn.sigmoid(pre)
    return sig * (1.0 + pre * (1.0 - sig))

def reference(latents, cotangent, timesteps, time_table, w_in, w_out, w_skip):
    outs_all = [[], [], [], []]
    grads_all = [[], [], [], []]
    width = w_in.shape[1]
    acc_first = [jnp.zeros((width, width), jnp.float32) for _ in range(4)]
    acc_second = [jnp.zeros((width, width), jnp.float32) for _ in range(4)]
    acc_side = [jnp.zeros((width, width), jnp.float32) for _ in range(4)]
    for micro_id in range(MICRO):
        action = latents[micro_id]
        skips = []
        saved = []
        for phase in range(4):
            bias = jnp.repeat(time_table[phase][timesteps[micro_id]].astype(jnp.float32), ROWS, axis=0)
            pre = jnp.dot(action, w_in[phase], preferred_element_type=jnp.float32) + bias
            if phase >= 2:
                side = skips[3 - phase]
                pre = pre + jnp.dot(side, w_skip[phase], preferred_element_type=jnp.float32)
            gated = jax.nn.silu(pre).astype(jnp.bfloat16)
            output = (action.astype(jnp.float32) + jnp.dot(gated, w_out[phase], preferred_element_type=jnp.float32)).astype(jnp.bfloat16)
            if phase < 2:
                skips.append(jnp.dot(output, w_skip[phase], preferred_element_type=jnp.float32).astype(jnp.bfloat16))
                left = output
            else:
                left = side
            saved.append((action, pre, gated, left))
            outs_all[phase].append(output)
            action = output
        upstream = cotangent[micro_id]
        dskips = [None, None]
        for phase in [3, 2, 1, 0]:
            action, pre, gated, left = saved[phase]
            if phase >= 2:
                total = upstream
            else:
                total = (upstream.astype(jnp.float32) + jnp.dot(dskips[phase], w_skip[phase].T, preferred_element_type=jnp.float32)).astype(jnp.bfloat16)
            d_pre = (jnp.dot(total, w_out[phase].T, preferred_element_type=jnp.float32) * silu_grad(pre)).astype(jnp.bfloat16)
            if phase >= 2:
                dskips[3 - phase] = jnp.dot(d_pre, w_skip[phase].T, preferred_element_type=jnp.float32).astype(jnp.bfloat16)
                right = d_pre
            else:
                right = dskips[phase]
            acc_first[phase] = acc_first[phase] + jnp.dot(action.T, d_pre, preferred_element_type=jnp.float32)
            acc_second[phase] = acc_second[phase] + jnp.dot(gated.T, total, preferred_element_type=jnp.float32)
            acc_side[phase] = acc_side[phase] + jnp.dot(left.T, right, preferred_element_type=jnp.float32)
            d_in = (total.astype(jnp.float32) + jnp.dot(d_pre, w_in[phase].T, preferred_element_type=jnp.float32)).astype(jnp.bfloat16)
            grads_all[phase].append(d_in)
            upstream = d_in
    phase_out = jnp.stack([jnp.stack(outs_all[phase]) for phase in range(4)])
    input_grads = jnp.stack([jnp.stack(grads_all[phase]) for phase in range(4)])
    return (phase_out, input_grads, jnp.stack(acc_first), jnp.stack(acc_second), jnp.stack(acc_side))
```

```python
import functools

import jax
import jax.numpy as jnp
from jax import lax
from jax.experimental import pallas as pl
from jax.experimental.pallas import tpu as pltpu
from jax.sharding import PartitionSpec as P

F32 = jnp.float32
BF16 = jnp.bfloat16
WITHIN = [(0, 1), (1, 0), (2, 3), (3, 2)]
UPWARD = [(0, 1), (1, 2), (2, 3), (3, 0)]
DOWNWARD = [(1, 0), (2, 1), (3, 2), (0, 3)]
VMEM = pl.BlockSpec(memory_space=pltpu.VMEM)
HBM = pl.BlockSpec(memory_space=pltpu.HBM)
SMEM = pl.BlockSpec(memory_space=pltpu.SMEM)
LANES = 128


def dot(a, b):
    return jnp.dot(a, b, preferred_element_type=F32)


def dot_t(a, b):
    return lax.dot_general(a, b, (((1,), (1,)), ((), ())), preferred_element_type=F32)


def sigmoid(v):
    return 1.0 / (1.0 + jnp.exp(-v))


def on_section(*slots):
    seg = lax.axis_index("segment")
    hit = seg == slots[0]
    for s in slots[1:]:
        hit = hit | (seg == s)
    return pl.when(hit)


def call(kernel, outs, args, name, flops, specs=None, scratch=(), limit=12):
    moved = sum(a.size * a.dtype.itemsize for a in args[:1])
    return pl.pallas_call(
        kernel,
        out_shape=[pltpu.VMEM(shape, dtype) for shape, dtype in outs],
        in_specs=specs or [VMEM] * len(args),
        out_specs=[VMEM] * len(outs),
        scratch_shapes=list(scratch),
        name=name,
        compiler_params=pltpu.CompilerParams(vmem_limit_bytes=limit * 2**20),
        cost_estimate=pl.CostEstimate(flops=flops, bytes_accessed=moved, transcendentals=0),
    )(*args)


def finish_forward(x, pre, wo_ref, pre_ref, gated_ref, out_ref):
    pre_ref[...] = pre
    gated = (pre * sigmoid(pre)).astype(BF16)
    gated_ref[...] = gated
    out_ref[...] = (x.astype(F32) + dot(gated, wo_ref[...])).astype(BF16)


def start_kernel(micro, steps_ref, x_ref, table_ref, wi_hbm, wo_hbm, ws_hbm,
                 wi_ref, wo_ref, ws_ref, bias_ref, pre_ref, gated_ref, out_ref, sems):
    loads = [
        pltpu.make_async_copy(src, dst, sems.at[k])
        for k, (src, dst) in enumerate(((wi_hbm, wi_ref), (wo_hbm, wo_ref), (ws_hbm, ws_ref)))
    ]
    for load in loads:
        load.start()
    count = table_ref.shape[0]
    row = lax.broadcasted_iota(jnp.int32, (bias_ref.shape[0], count), 0)
    col = lax.broadcasted_iota(jnp.int32, (bias_ref.shape[0], count), 1)
    wanted = jnp.full(row.shape, -1, jnp.int32)
    for m in range(micro):
        wanted = jnp.where(row == m, steps_ref[m, 0], wanted)
    bias_ref[...] = dot((col == wanted).astype(F32).astype(BF16), table_ref[...])
    loads[0].wait()
    loads[1].wait()

    @on_section(0)
    def _():
        x = x_ref[...]
        finish_forward(x, dot(x, wi_ref[...]) + bias_ref[0:1, :], wo_ref, pre_ref, gated_ref, out_ref)

    loads[2].wait()


def forward_kernel(slot, m, x_ref, bias_ref, wi_ref, wo_ref, pre_ref, gated_ref, out_ref):
    @on_section(slot)
    def _():
        x = x_ref[...]
        pre = dot(x, wi_ref[...]) + bias_ref[m : m + 1, :]
        finish_forward(x, pre, wo_ref, pre_ref, gated_ref, out_ref)


def part_kernel(slot, m, a_ref, bias_ref, w_ref, part_ref):
    @on_section(slot)
    def _():
        part_ref[...] = dot(a_ref[...], w_ref[...]) + bias_ref[m : m + 1, :]


def forward_part_kernel(slot, x_ref, a_ref, part_ref, w_ref, wo_ref, pre_ref, gated_ref, out_ref):
    @on_section(slot)
    def _():
        pre = part_ref[...] + dot(a_ref[...], w_ref[...])
        finish_forward(x_ref[...], pre, wo_ref, pre_ref, gated_ref, out_ref)


def product_kernel(slot, transposed, a_ref, w_ref, o_ref):
    @on_section(slot)
    def _():
        o_ref[...] = (dot_t if transposed else dot)(a_ref[...], w_ref[...]).astype(o_ref.dtype)


def silu_grad(pre):
    sig = sigmoid(pre)
    return sig * (1.0 + pre * (1.0 - sig))


def last_backward_kernel(slot, total_ref, back_ref, pre_ref, wi_ref, d_pre_ref, d_in_ref):
    @on_section(slot)
    def _():
        d_pre = (back_ref[...] * silu_grad(pre_ref[...])).astype(BF16)
        d_pre_ref[...] = d_pre
        d_in_ref[...] = (total_ref[...].astype(F32) + dot_t(d_pre, wi_ref[...])).astype(BF16)


def mid_backward_kernel(slot, total_ref, pre_ref, wo_ref, ws_ref, d_pre_ref, dskip_ref):
    @on_section(slot)
    def _():
        d_pre = (dot_t(total_ref[...], wo_ref[...]) * silu_grad(pre_ref[...])).astype(BF16)
        d_pre_ref[...] = d_pre
        dskip_ref[...] = dot_t(d_pre, ws_ref[...]).astype(BF16)


def d_in_kernel(slot, total_ref, d_pre_ref, wi_ref, d_in_ref):
    @on_section(slot)
    def _():
        d_in_ref[...] = (total_ref[...].astype(F32) + dot_t(d_pre_ref[...], wi_ref[...])).astype(BF16)


def down_backward_kernel(slot, up_ref, side_ref, pre_ref, wo_ref, wi_ref, total_ref, d_pre_ref, d_in_ref):
    @on_section(slot)
    def _():
        total = (up_ref[...].astype(F32) + side_ref[...]).astype(BF16)
        total_ref[...] = total
        d_pre = (dot_t(total, wo_ref[...]) * silu_grad(pre_ref[...])).astype(BF16)
        d_pre_ref[...] = d_pre
        d_in_ref[...] = (total.astype(F32) + dot_t(d_pre, wi_ref[...])).astype(BF16)


def block_order(devices):
    order = [0]
    step = devices // 2
    while step > 1:
        order = [r | step for r in order] + order
        step //= 2
    return order


def lefts_kernel(slots, devices, micro, lefts, *refs):
    count = lefts * micro
    sources = [refs[k * count : (k + 1) * count] for k in range(len(slots))]
    near_ref, far_ref, turned, gathered = refs[len(slots) * count :]
    rows, width = sources[0][0].shape
    block = width // devices
    half = width // 2
    dp_id = lax.axis_index("dp")
    for slot, refs_here in zip(slots, sources):
        @on_section(slot)
        def _(refs_here=refs_here):
            for i in range(lefts):
                for m in range(micro):
                    turned[...] = refs_here[i * micro + m][...].astype(F32).T
                    for far in (0, 1):
                        for p, mask in enumerate(block_order(devices)):
                            at = pl.multiple_of(jnp.bitwise_xor(dp_id, mask ^ far) * block, 8)
                            gathered[pl.ds(p * block, block), :] = turned[pl.ds(at, block), :]
                        if far:
                            for j in range(half // LANES):
                                far_ref[
                                    pl.ds(m * rows, rows), pl.ds(i * half + j * LANES, LANES)
                                ] = gathered[pl.ds(j * LANES, LANES), :].astype(BF16)
                        else:
                            near_ref[i, :, pl.ds(m * rows, rows)] = gathered[...].astype(BF16)


def pack_lefts(slots, values, devices, micro, name):
    lefts = len(values[0]) // micro
    rows, width = values[0][0].shape
    half = width // 2
    return call(
        functools.partial(lefts_kernel, slots, devices, micro, lefts),
        [((lefts, half, micro * rows), BF16), ((micro * rows, lefts * half), BF16)],
        [v for vs in values for v in vs],
        name,
        10**9,
        scratch=[pltpu.VMEM((width, rows), F32), pltpu.VMEM((half, rows), F32)],
    )


def grad_kernel(picks, rows, near_a, far_a, near_b, far_b, right_ref, right_far, send_ref, keep_ref,
                left_ref, both_ref):
    n, width = right_ref.shape
    half = near_a.shape[1]
    for slots, i, near, far in ((((0, 1), picks[0], near_a, far_a)), ((2, 3), picks[1], near_b, far_b)):
        @on_section(*slots)
        def _(i=i, near=near, far=far):
            left_ref[:, pl.ds(0, n)] = near[i]
            for m in range(n // rows):
                for j in range(half // LANES):
                    left_ref[pl.ds(j * LANES, LANES), pl.ds(n + m * rows, rows)] = far[
                        pl.ds(m * rows, rows), pl.ds(i * half + j * LANES, LANES)
                    ]
    both_ref[pl.ds(0, n), :] = right_ref[...]
    both_ref[pl.ds(n, n), :] = right_far[...]
    cut = half // 2
    send_ref[...] = dot(left_ref[pl.ds(0, cut), :], both_ref[...]).astype(BF16)
    keep_ref[...] = dot(left_ref[pl.ds(cut, cut), :], both_ref[...])


def flip(x, bit):
    devices = lax.axis_size("dp")
    return lax.ppermute(x, "dp", [(i, i ^ bit) for i in range(devices)])


def grad_sum(lefts_a, lefts_b, picks, right, right_far, rows, devices, name):
    n, width = right.shape
    half = width // 2
    near, keep = call(
        functools.partial(grad_kernel, picks, rows),
        [((half // 2, width), BF16), ((half // 2, width), F32)],
        [*lefts_a, *lefts_b, right, right_far],
        name,
        4 * half * width * n,
        scratch=[pltpu.VMEM((half, 2 * n), BF16), pltpu.VMEM((2 * n, width), BF16)],
    )
    step = 2
    while True:
        total = keep + flip(near, step).astype(F32)
        step *= 2
        if step == devices:
            return total
        cut = total.shape[0] // 2
        near, keep = total[:cut].astype(BF16), total[cut:]


def body(latents, cotangent, timesteps, time_table, w_in, w_out, w_skip):
    seg = lax.axis_index("segment")
    devices = lax.axis_size("dp")
    micro, rows, width = latents.shape
    ms = range(micro)
    flops = 2 * rows * width * width
    act, wide = ((rows, width), BF16), ((rows, width), F32)
    weight = ((width, width), BF16)
    send = lambda x, pairs: lax.ppermute(x, "segment", pairs)

    def product(slot, a, w, transposed, out, name):
        return call(functools.partial(product_kernel, slot, transposed), [out], [a, w], name, flops)[0]

    x0 = [latents[m] for m in ms]
    cot = [cotangent[m] for m in ms]
    started = call(
        functools.partial(start_kernel, micro),
        [weight, weight, weight, ((16, width), F32), wide, act, act],
        [timesteps, x0[0], time_table[0], w_in[0], w_out[0], w_skip[0]],
        "start",
        2 * flops,
        specs=[SMEM, VMEM, VMEM, HBM, HBM, HBM],
        scratch=[pltpu.SemaphoreType.DMA((3,))],
    )
    wi, wo, ws, bias = started[:4]

    def forward(slot, m, x):
        return call(
            functools.partial(forward_kernel, slot, m), [wide, act, act], [x, bias, wi, wo],
            f"forward{slot}", 2 * flops)

    def part(slot, m, a, w):
        return call(functools.partial(part_kernel, slot, m), [wide], [a, bias, w], f"part{slot}", flops)[0]

    def forward_part(slot, x, a, given, w):
        return call(
            functools.partial(forward_part_kernel, slot), [wide, act, act], [x, a, given, w, wo],
            f"forward{slot}", 2 * flops)

    pre, gated, out = [[[None] * micro for _ in range(4)] for _ in range(3)]
    d_pre, d_in, total = [[[None] * micro for _ in range(4)] for _ in range(3)]
    xs = [x0] + [[None] * micro for _ in range(3)]
    skip_far = [[None] * micro for _ in range(2)]
    dskip_far = [[None] * micro for _ in range(2)]
    total[3] = cot

    for m in ms:
        pre[0][m], gated[0][m], out[0][m] = started[4:] if m == 0 else forward(0, m, x0[m])
        xs[1][m] = send(out[0][m], WITHIN)
        skip_far[0][m] = send(product(0, out[0][m], ws, False, act, "skip0"), DOWNWARD)
    for m in ms:
        pre[1][m], gated[1][m], out[1][m] = forward(1, m, xs[1][m])
        xs[2][m] = send(out[1][m], UPWARD)
        skip_far[1][m] = send(product(1, out[1][m], ws, False, act, "skip1"), UPWARD)
    back = [product(3, cot[m], wo, True, wide, "back3") for m in ms]
    lefts_a = pack_lefts(
        (0, 1), [[*xs[s], *gated[s], *out[s]] for s in (0, 1)], devices, micro, "lefts_down")
    far_a = flip(lefts_a[1], 1)
    dskip0 = [None] * micro
    for m in ms:
        given = part(2, m, xs[2][m], wi)
        pre[2][m], gated[2][m], out[2][m] = forward_part(2, xs[2][m], skip_far[1][m], given, ws)
        xs[3][m] = send(out[2][m], WITHIN)
    for m in ms:
        given = part(3, m, skip_far[0][m], ws)
        pre[3][m], gated[3][m], out[3][m] = forward_part(3, xs[3][m], xs[3][m], given, wi)
        d_pre[3][m], d_in[3][m] = call(
            functools.partial(last_backward_kernel, 3), [act, act], [cot[m], back[m], pre[3][m], wi],
            "backward3", flops)
        total[2][m] = send(d_in[3][m], WITHIN)
        dskip_far[0][m] = send(product(3, d_pre[3][m], ws, True, act, "dskip0"), UPWARD)
    up1 = [None] * micro
    for m in ms:
        d_pre[2][m], dskip1 = call(
            functools.partial(mid_backward_kernel, 2), [act, act], [total[2][m], pre[2][m], wo, ws],
            "backward2", 2 * flops)
        dskip_far[1][m] = send(dskip1, DOWNWARD)
        d_in[2][m] = call(
            functools.partial(d_in_kernel, 2), [act], [total[2][m], d_pre[2][m], wi], "d_in2", flops)[0]
        up1[m] = send(d_in[2][m], DOWNWARD)
    lefts_b1 = pack_lefts((2, 3), [gated[s] for s in (2, 3)], devices, micro, "lefts_up1")
    far_b1 = flip(lefts_b1[1], 1)
    lefts_b2 = pack_lefts(
        (2, 3), [[*xs[s], *skip_far[3 - s]] for s in (2, 3)], devices, micro, "lefts_up2")
    far_b2 = flip(lefts_b2[1], 1)
    up0 = [None] * micro
    for m in ms:
        side = product(1, dskip_far[1][m], ws, True, wide, "side1")
        total[1][m], d_pre[1][m], d_in[1][m] = call(
            functools.partial(down_backward_kernel, 1), [act, act, act],
            [up1[m], side, pre[1][m], wo, wi], "backward1", 2 * flops)
        up0[m] = send(d_in[1][m], WITHIN)
    for m in ms:
        side = product(0, dskip_far[0][m], ws, True, wide, "side0")
        total[0][m], d_pre[0][m], d_in[0][m] = call(
            functools.partial(down_backward_kernel, 0), [act, act, act],
            [up0[m], side, pre[0][m], wo, wi], "backward0", 2 * flops)

    def choose(values):
        return jnp.concatenate(
            [
                jnp.where(
                    seg < 2,
                    jnp.where(seg == 0, values[0][m], values[1][m]),
                    jnp.where(seg == 2, values[2][m], values[3][m]),
                )
                for m in ms
            ],
            axis=0,
        )

    right1 = choose([dskip_far[0], dskip_far[1], total[2], total[3]])
    right2 = choose([total[0], total[1], d_pre[2], d_pre[3]])
    right3 = choose(d_pre)
    far1, far2, far3 = flip(right1, 1), flip(right2, 1), flip(right3, 1)
    left_a = (lefts_a[0], far_a)
    left_b1, left_b2 = (lefts_b1[0], far_b1), (lefts_b2[0], far_b2)
    first = grad_sum(left_a, left_b1, (2, 0), right1, far1, rows, devices, "grad1")
    second = grad_sum(left_a, left_b2, (1, 0), right2, far2, rows, devices, "grad2")
    third = grad_sum(left_a, left_b2, (0, 1), right3, far3, rows, devices, "grad3")
    down = seg < 2
    return (
        choose(out).reshape(1, micro, rows, width),
        choose(d_in).reshape(1, micro, rows, width),
        jnp.where(down, third, second)[None],
        jnp.where(down, second, first)[None],
        jnp.where(down, first, third)[None],
    )


def solution(mesh):
    in_specs = (
        P(None, "dp", None),
        P(None, "dp", None),
        P(None, "dp"),
        P("segment", None, None),
        P("segment", None, None),
        P("segment", None, None),
        P("segment", None, None),
    )
    out_specs = (
        P("segment", None, "dp", None),
        P("segment", None, "dp", None),
        P("segment", "dp", None),
        P("segment", "dp", None),
        P("segment", "dp", None),
    )
    return jax.shard_map(body, mesh=mesh, in_specs=in_specs, out_specs=out_specs, check_vma=False)
```

```python
import functools
import types

import jax
import jax.numpy as jnp
from jax import lax
from jax.experimental import pallas as pl
from jax.experimental.pallas import tpu as pltpu
from jax.sharding import PartitionSpec as P

F32 = jnp.float32
BF16 = jnp.bfloat16
WITHIN = [(0, 1), (1, 0), (2, 3), (3, 2)]
UPWARD = [(0, 1), (1, 2), (2, 3), (3, 0)]
DOWNWARD = [(1, 0), (2, 1), (3, 2), (0, 3)]
DOWN, UP = (0, 1), (2, 3)
VMEM = pl.BlockSpec(memory_space=pltpu.VMEM)
HBM = pl.BlockSpec(memory_space=pltpu.HBM)
SMEM = pl.BlockSpec(memory_space=pltpu.SMEM)
ANY = pl.BlockSpec(memory_space=pl.ANY)
LANES = 128


def dot(a, b):
    return jnp.dot(a, b, preferred_element_type=F32)


def sigmoid(v):
    return 1.0 / (1.0 + jnp.exp(-v))


def silu_grad(pre):
    sig = sigmoid(pre)
    return sig * (1.0 + pre * (1.0 - sig))


def on_section(*slots):
    seg = lax.axis_index("segment")
    hit = seg == slots[0]
    for s in slots[1:]:
        hit = hit | (seg == s)
    return pl.when(hit)


class Chain:
    def __init__(self):
        self.stores = {}

    def call(self, kernel, args, outs, name, new=(), drop=(), specs=None, scratch=(), after=(), to_hbm=()):
        for key in drop:
            self.stores.pop(key)
        held = list(self.stores)
        made = dict(new)
        ins, extra = len(args), len(after)

        def run(*refs):
            here = refs[ins + extra + len(held) :]
            results, here = here[: len(outs)], here[len(outs) :]
            names = held + list(made)
            kernel(
                types.SimpleNamespace(**dict(zip(names, here))),
                *refs[:ins],
                *results,
                *here[len(names) :],
            )

        in_vmem = lambda a: pltpu.with_memory_space_constraint(a, pltpu.VMEM)
        specs = list(specs or [VMEM] * ins)
        values = [
            pltpu.with_memory_space_constraint(a, pltpu.HBM) if spec is HBM else a
            for a, spec in zip(args, specs)
        ]
        stores = [self.stores[key] for key in held]
        shapes = list(outs) + [(a.shape, a.dtype) for a in stores] + list(made.values())
        results = pl.pallas_call(
            run,
            out_shape=[
                (pltpu.HBM if k in to_hbm else pltpu.VMEM)(shape, dtype) for k, (shape, dtype) in enumerate(shapes)
            ],
            in_specs=specs + [ANY] * extra + [VMEM] * len(held),
            out_specs=[HBM if k in to_hbm else VMEM for k in range(len(shapes))],
            scratch_shapes=list(scratch),
            input_output_aliases={ins + extra + k: len(outs) + k for k in range(len(held))},
            name=name,
            compiler_params=pltpu.CompilerParams(vmem_limit_bytes=12 * 2**20),
            cost_estimate=pl.CostEstimate(flops=1000, bytes_accessed=1000, transcendentals=0),
        )(*values, *after, *[in_vmem(a) for a in stores])
        self.stores = dict(zip(held + list(made), results[len(outs) :]))
        return results[: len(outs)]


def pieces(source, target, sems, first, count=4):
    rows = target.shape[0] // count
    return [
        pltpu.make_async_copy(
            source.at[pl.ds(k * rows, rows)], target.at[pl.ds(k * rows, rows)], sems.at[first + k]
        )
        for k in range(count)
    ]


def place(m, rows):
    return pl.ds(m * rows, rows)


def finish_forward(s, at, x, pre):
    s.pre[at, :] = pre
    gated = (pre * sigmoid(pre)).astype(BF16)
    s.gated[at, :] = gated
    out = (x.astype(F32) + dot(gated, s.wo[...])).astype(BF16)
    s.out[at, :] = out
    return out


def start_kernel(micro, rows, s, steps_ref, x_hbm, cot_hbm, table_hbm, wi_hbm, wo_hbm, out_ref, table_ref, sems):
    load_x = [pltpu.make_async_copy(x_hbm.at[m], s.x.at[place(m, rows)], sems.at[m]) for m in range(micro)]
    load_cot = [
        pltpu.make_async_copy(cot_hbm.at[m], s.total.at[place(m, rows)], sems.at[micro + m]) for m in range(micro)
    ]
    load_table = [pltpu.make_async_copy(table_hbm.at[0], table_ref, sems.at[2 * micro])]
    load_wi = pieces(wi_hbm.at[0], s.wi, sems, 2 * micro + 1)
    load_wo = pieces(wo_hbm.at[0], s.wo, sems, 2 * micro + 5)
    for load in load_table + load_x + load_wi + load_wo + load_cot:
        load.start()
    count = table_ref.shape[0]
    row = lax.broadcasted_iota(jnp.int32, (s.bias.shape[0], count), 0)
    col = lax.broadcasted_iota(jnp.int32, (s.bias.shape[0], count), 1)
    wanted = jnp.full(row.shape, -1, jnp.int32)
    for m in range(micro):
        wanted = jnp.where(row == m, steps_ref[m, 0], wanted)
    chosen = (col == wanted).astype(F32).astype(BF16)
    for load in load_table:
        load.wait()
    s.bias[...] = dot(chosen, table_ref[...])
    for load in load_x + load_wi:
        load.wait()
    at = place(0, rows)

    @on_section(0)
    def _():
        s.pre[at, :] = dot(s.x[at, :], s.wi[...]) + s.bias[0:1, :]

    for load in load_wo:
        load.wait()

    @on_section(0)
    def _():
        out_ref[...] = finish_forward(s, at, s.x[at, :], s.pre[at, :])

    for load in load_cot:
        load.wait()


def first_skip_kernel(rows, s, ws_hbm, skip_ref, sems):
    loads = pieces(ws_hbm.at[0], s.ws, sems, 0)
    for load in loads:
        load.start()
    for load in loads:
        load.wait()

    @on_section(0)
    def _():
        skip_ref[...] = dot(s.out[place(0, rows), :], s.ws[...]).astype(BF16)


def skip_kernel(m, rows, s, skip_ref):
    @on_section(0)
    def _():
        skip_ref[...] = dot(s.out[place(m, rows), :], s.ws[...]).astype(BF16)


def forward0_kernel(m, rows, s, out_ref):
    @on_section(0)
    def _():
        at = place(m, rows)
        x = s.x[at, :]
        out_ref[...] = finish_forward(s, at, x, dot(x, s.wi[...]) + s.bias[m : m + 1, :])


def forward1_kernel(m, rows, s, x_ref, pair_ref):
    @on_section(1)
    def _():
        at = place(m, rows)
        x = x_ref[...]
        s.x[at, :] = x
        out = finish_forward(s, at, x, dot(x, s.wi[...]) + s.bias[m : m + 1, :])
        pair_ref[pl.ds(0, rows), :] = out
        pair_ref[pl.ds(rows, rows), :] = dot(out, s.ws[...]).astype(BF16)


def forward2_kernel(m, rows, s, pair_ref, out_ref):
    @on_section(2)
    def _():
        at = place(m, rows)
        x = pair_ref[pl.ds(0, rows), :]
        skip = pair_ref[pl.ds(rows, rows), :]
        s.x[at, :] = x
        s.side[at, :] = skip
        pre = dot(x, s.wi[...]) + dot(skip, s.ws[...]) + s.bias[m : m + 1, :]
        out_ref[...] = finish_forward(s, at, x, pre)


def add_skip_kernel(m, rows, s, skip_ref):
    @on_section(3)
    def _():
        at = place(m, rows)
        skip = skip_ref[...]
        s.side[at, :] = skip
        s.part[at, :] = dot(skip, s.ws[...]) + s.bias[m : m + 1, :]


def turn_kernel(slots, s):
    @on_section(*slots)
    def _():
        s.wo_t[...] = s.wo[...].T
        s.wi_t[...] = s.wi[...].T
        s.ws_t[...] = s.ws[...].T

    if 3 in slots:
        @on_section(3)
        def _():
            s.back[...] = dot(s.total[...], s.wo_t[...])


def turn3_kernel(m, rows, s, x_ref, d_in_ref):
    @on_section(3)
    def _():
        at = place(m, rows)
        x = x_ref[...]
        s.x[at, :] = x
        pre = s.part[at, :] + dot(x, s.wi[...])
        finish_forward(s, at, x, pre)
        d_pre = (s.back[at, :] * silu_grad(pre)).astype(BF16)
        s.d_pre[at, :] = d_pre
        d_in = (s.total[at, :].astype(F32) + dot(d_pre, s.wi_t[...])).astype(BF16)
        s.d_in[at, :] = d_in
        d_in_ref[...] = d_in


def dskip_kernel(m, rows, s, dskip_ref):
    @on_section(3)
    def _():
        dskip_ref[...] = dot(s.d_pre[place(m, rows), :], s.ws_t[...]).astype(BF16)


def finish_backward(s, at, total):
    s.total[at, :] = total
    d_pre = (dot(total, s.wo_t[...]) * silu_grad(s.pre[at, :])).astype(BF16)
    s.d_pre[at, :] = d_pre
    d_in = (total.astype(F32) + dot(d_pre, s.wi_t[...])).astype(BF16)
    s.d_in[at, :] = d_in
    return d_pre, d_in


def backward2_kernel(m, rows, s, total_ref, pair_ref):
    @on_section(2)
    def _():
        d_pre, d_in = finish_backward(s, place(m, rows), total_ref[...])
        pair_ref[pl.ds(0, rows), :] = d_in
        pair_ref[pl.ds(rows, rows), :] = dot(d_pre, s.ws_t[...]).astype(BF16)


def down_backward(m, rows, s, up):
    at = place(m, rows)
    total = (up.astype(F32) + dot(s.side[at, :], s.ws_t[...])).astype(BF16)
    return finish_backward(s, at, total)[1]


def backward1_kernel(m, rows, s, pair_ref, d_in_ref):
    @on_section(1)
    def _():
        s.side[place(m, rows), :] = pair_ref[pl.ds(rows, rows), :]
        d_in_ref[...] = down_backward(m, rows, s, pair_ref[pl.ds(0, rows), :])


def backward0_kernel(m, rows, s, up_ref):
    @on_section(0)
    def _():
        down_backward(m, rows, s, up_ref[...])


def block_order(steps):
    order = [0]
    for step in reversed(steps):
        order = [r | step for r in order] + order
    return order


def lefts_kernel(slots, devices, micro, rows, names, shared, steps, s, far_ref, turned, gathered):
    width = turned.shape[0]
    block, half = width // devices, width // 2
    dp_id = lax.axis_index("dp")

    @on_section(*slots)
    def _():
        for i, (store, name) in enumerate(names):
            for m in range(micro):
                turned[...] = getattr(s, name)[place(m, rows), :].astype(F32).T
                for far in (0, shared):
                    for p, mask in enumerate(block_order(steps)):
                        at = pl.multiple_of(jnp.bitwise_xor(dp_id, mask ^ far) * block, 8)
                        gathered[pl.ds(p * block, block), :] = turned[pl.ds(at, block), :]
                    if far:
                        for j in range(half // LANES):
                            far_ref[place(m, rows), pl.ds(i * half + j * LANES, LANES)] = gathered[
                                pl.ds(j * LANES, LANES), :
                            ].astype(BF16)
                    else:
                        s.near[store, :, place(m, rows)] = gathered[...].astype(BF16)


def right_kernel(m, rows, s, dskip_ref, packed):
    at = place(m, rows)

    @on_section(0)
    def _():
        s.side[at, :] = dskip_ref[...]
        packed[...] = dskip_ref[...]

    @on_section(1)
    def _():
        packed[...] = s.side[at, :]

    @on_section(2, 3)
    def _():
        packed[...] = s.total[at, :]


def pack_kernel(m, rows, down, up, s, packed):
    for slots, name in ((DOWN, down), (UP, up)):
        if name:
            @on_section(*slots)
            def _(name=name):
                packed[...] = getattr(s, name)[...] if m is None else getattr(s, name)[place(m, rows), :]


def turned_order(count):
    order = [0]
    step = 1
    while step < count:
        order = [p * 2 for p in order] + [p * 2 + 1 for p in order]
        step *= 2
    return order


def grad_kernel(parts, block, rows, micro, down, up, keeps, dumps, s, far_down, far_up, *refs):
    *refs, left_ref, right_ref, sum_ref, sems = refs
    targets = refs[len(refs) - len(dumps) :]
    refs = refs[: len(refs) - len(dumps)]
    fars, sends = refs[: -len(parts)], refs[-len(parts) :]
    copies = [
        pltpu.make_async_copy(getattr(s, name).at[place(m, rows)], target.at[0, m], sems.at[k * micro + m])
        for k, (name, target) in enumerate(zip(dumps, targets))
        for m in range(micro)
    ]
    for copy in copies:
        copy.start()
    n = micro * rows
    half = left_ref.shape[0]
    for slots, (i, column, name, first), far in ((DOWN, down, far_down), (UP, up, far_up)):
        @on_section(*slots)
        def _(i=i, column=column, name=name, first=first, far=far):
            left_ref[:, pl.ds(0, n)] = s.near[i]
            right_ref[pl.ds(0, n), :] = getattr(s, name)[...]
            at = n
            for k in range(first, first + micro):
                if at < 2 * n:
                    size = fars[k].shape[0]
                    right_ref[pl.ds(at, size), :] = fars[k][...]
                    at += size
            for m in range(micro):
                for j in range(half // LANES):
                    left_ref[pl.ds(j * LANES, LANES), pl.ds(n + m * rows, rows)] = far[
                        place(m, rows), pl.ds(column * half + j * LANES, LANES)
                    ]

    cut = half // 2
    for (start, size, turned), send_ref, keep in zip(parts, sends, keeps):
        keep_ref = getattr(s, keep)
        right = right_ref[:, pl.ds(start, size)]
        if not turned:
            send_ref[...] = dot(left_ref[pl.ds(0, cut), :], right).astype(BF16)
            keep_ref[...] = dot(left_ref[pl.ds(cut, cut), :], right)
        else:
            sum_ref[:, pl.ds(0, size)] = dot(left_ref[...], right)
            order = turned_order(half // block)
            picked = [sum_ref[pl.ds(p * block, block), pl.ds(0, size)] for p in order]
            middle = len(order) // 2
            send_ref[...] = jnp.concatenate(picked[:middle], axis=0).astype(BF16)
            keep_ref[...] = jnp.concatenate(picked[middle:], axis=0)
    for copy in copies:
        copy.wait()


def merge_kernel(keep, rest, s, far_ref, near_ref):
    cut = near_ref.shape[0]
    total = getattr(s, keep)[...] + far_ref[...].astype(F32)
    near_ref[...] = total[:cut].astype(BF16)
    getattr(s, rest)[...] = total[cut:]


def flip(x, bit, sections=None):
    devices = lax.axis_size("dp")
    if sections is None:
        return lax.ppermute(x, "dp", [(i, i ^ bit) for i in range(devices)])
    pairs = [(s * devices + i, s * devices + (i ^ bit)) for s in sections for i in range(devices)]
    return lax.ppermute(x, ("segment", "dp"), pairs)


def body(latents, cotangent, timesteps, time_table, w_in, w_out, w_skip):
    devices = lax.axis_size("dp")
    last = lax.axis_size("segment") - 1
    micro, rows, width = latents.shape
    ms = range(micro)
    n, half, block = micro * rows, width // 2, width // devices
    act, pair = ((rows, width), BF16), ((2 * rows, width), BF16)
    whole, weight = ((n, width), BF16), ((width, width), BF16)
    chain = Chain()
    send = lambda x, pairs: lax.ppermute(x, "segment", pairs)
    bound = functools.partial

    bits = [1 << k for k in range(devices.bit_length() - 1)]
    by_y, by_z = (bits[0], bits[1:]), (bits[1], bits[:1] + bits[2:])

    def lefts(slots, names, name, way, after=(), drop=(), tall=n):
        shared, steps = way
        far = chain.call(
            bound(lefts_kernel, slots, devices, micro, rows, names, shared, steps), [],
            [((tall, len(names) * half), BF16)], name,
            scratch=[pltpu.VMEM((width, rows), F32), pltpu.VMEM((half, rows), F32)], after=after, drop=drop)[0]
        return flip(far, shared, slots)

    def share(m, down, up, name, way, sections=None, after=()):
        shape = ((n if m is None else rows, width), BF16)
        packed = chain.call(bound(pack_kernel, m, rows, down, up), [], [shape], name, after=after)[0]
        return flip(packed, way[0], sections)

    def grad(parts, way, down, up, far_down, far_up, fars, name, dumps=(), after=()):
        keeps = [f"{name}_{k}" for k in range(len(parts))]
        sends = chain.call(
            bound(grad_kernel, parts, block, rows, micro, down, up, keeps, dumps), [far_down, far_up, *fars],
            [((half // 2, size), BF16) for _, size, _ in parts] + [((1, micro, rows, width), BF16)] * len(dumps), name,
            new=[(key, ((half // 2, size), F32)) for key, (_, size, _) in zip(keeps, parts)],
            scratch=[
                pltpu.VMEM((half, 2 * n), BF16), pltpu.VMEM((2 * n, width), BF16), pltpu.VMEM((half, width), F32),
                pltpu.SemaphoreType.DMA((2 * micro,)),
            ],
            to_hbm=[len(parts) + k for k in range(len(dumps))], after=after)
        states = []
        for (_, _, turned), key, out in zip(parts, keeps, sends):
            left = way[1][::-1] if turned else way[1]
            states.append((key, flip(out, left[0]), left[1:]))
        return (states, *sends[len(parts) :])

    def merge(state, after=()):
        key, far, steps = state
        if not steps:
            return state
        rest = key + "m"
        cut, size = far.shape[0] // 2, far.shape[1]
        near = chain.call(
            bound(merge_kernel, key, rest), [far], [((cut, size), BF16)], "merge",
            new=[(rest, ((cut, size), F32))], after=after)[0]
        chain.stores.pop(key)
        return rest, flip(near, steps[0]), steps[1:]

    names16 = ("x", "gated", "out", "side", "total", "d_pre", "d_in")
    stores = [(k, weight) for k in ("wi", "wo", "ws", "wi_t", "wo_t", "ws_t")]
    stores += [(k, whole) for k in names16] + [(k, ((n, width), F32)) for k in ("pre", "part", "back")]
    stores += [("bias", ((16, width), F32)), ("near", ((3, half, n), BF16))]
    x1, skip0, far1, x3, total2, dskip0, far2, up0 = ([None] * micro for _ in range(8))

    out = chain.call(
        bound(start_kernel, micro, rows), [timesteps, latents, cotangent, time_table, w_in, w_out], [act], "start",
        new=stores, specs=[SMEM, HBM, HBM, HBM, HBM, HBM],
        scratch=[pltpu.VMEM(time_table.shape[1:], BF16), pltpu.SemaphoreType.DMA((2 * micro + 9,))])[0]
    x1[0] = send(out, WITHIN)
    skip = chain.call(
        bound(first_skip_kernel, rows), [w_skip], [act], "skip0", specs=[HBM],
        scratch=[pltpu.SemaphoreType.DMA((4,))])[0]
    skip0[0] = send(skip, [(0, last)])
    for m in ms[1:]:
        x1[m] = send(chain.call(bound(forward0_kernel, m, rows), [], [act], "forward0")[0], WITHIN)
    for m in ms[1:]:
        skip0[m] = send(chain.call(bound(skip_kernel, m, rows), [], [act], "skip0")[0], [(0, last)])
    chain.call(bound(turn_kernel, UP), [], [], "turn_up")
    for m in ms:
        far1[m] = send(chain.call(bound(forward1_kernel, m, rows), [x1[m]], [pair], "forward1")[0], UPWARD)

    tall = n + (n // 2 + 16)
    down_z = lefts(DOWN, [(1, "gated")], "lefts_down", by_z, tall=2 * tall)
    down_y = lefts(DOWN, [(2, "out"), (0, "x")], "lefts_down", by_y, tall=tall)

    def forward2(m):
        chain.call(bound(add_skip_kernel, m, rows), [skip0[m]], [], "part3")
        x3[m] = send(chain.call(bound(forward2_kernel, m, rows), [far1[m]], [act], "forward2")[0], WITHIN)

    def turn3(m):
        total2[m] = send(chain.call(bound(turn3_kernel, m, rows), [x3[m]], [act], "turn3")[0], WITHIN)
        dskip0[m] = send(chain.call(bound(dskip_kernel, m, rows), [], [act], "dskip0")[0], [(last, 0)])

    def backward2(m):
        far2[m] = send(
            chain.call(bound(backward2_kernel, m, rows), [total2[m]], [pair], "backward2")[0], DOWNWARD)

    forward2(0)
    chain.call(bound(turn_kernel, DOWN), [], [], "turn_down")
    turn3(0)
    for m in ms[1:]:
        forward2(m)
        backward2(m - 1)
        turn3(m)
    backward2(micro - 1)
    up_y = lefts(UP, [(1, "gated")], "lefts_up", by_y, [dskip0[0], down_z, down_y], ("part", "back"))
    up_z = lefts(UP, [(0, "x")], "lefts_up", by_z, tall=2 * n)
    up_y2 = lefts(UP, [(2, "side")], "lefts_up", by_y)
    for key in ("x", "gated"):
        chain.stores.pop(key)
    rights1 = []
    for m in ms:
        up0[m] = send(
            chain.call(bound(backward1_kernel, m, rows), [far2[m]], [act], "backward1")[0],
            WITHIN)
        packed = chain.call(
            bound(right_kernel, m, rows), [dskip0[m]], [act], "right1", after=rights1 or [up_y])[0]
        rights1.append(flip(packed, by_y[0]))
        chain.call(bound(backward0_kernel, m, rows), [up0[m]], [], "backward0")
    right2 = share(None, "total", "d_pre", "right2", by_z)
    right3 = share(None, "d_pre", "d_pre", "right3", by_y)
    for key in ("wi", "wo", "ws", "wi_t", "wo_t", "ws_t", "pre", "bias"):
        chain.stores.pop(key)

    cut = width // 2
    mixed = [(0, cut, False), (cut, width - cut, True)]
    plain = [(0, cut, False), (cut, width - cut, False)]
    (first,) = grad(
        mixed, by_y, (2, 0, "side", 0), (1, 0, "total", 0), down_y, up_y, rights1, "grad1", after=[up_z])
    (second,) = grad(plain, by_z, (1, 0, "total", 0), (0, 0, "d_pre", 0), down_z, up_z, [right2], "grad2")
    third, phase_out, input_grads = grad(
        plain, by_y, (0, 1, "d_pre", 0), (2, 0, "d_pre", 0), down_y, up_y2, [right3], "grad3", ("out", "d_in"))
    for key in ("side", "total", "d_pre", "near", "out", "d_in"):
        chain.stores.pop(key)
    states = first[::-1] + second + third
    while states[0][2]:
        done = []
        for k, state in enumerate(states):
            after = [s[1] for s in done[k - 3 : k - 1]] if k in (3, 5) else []
            done.append(merge(state, after))
        states = done
    states = states[1::-1] + states[2:]
    sums = [chain.stores[key] + far.astype(F32) for key, far, _ in states]
    first, second, third = (jnp.concatenate(sums[k : k + 2], axis=1) for k in (0, 2, 4))
    down = lax.axis_index("segment") < 2
    return (
        phase_out,
        input_grads,
        jnp.where(down, third, second)[None],
        jnp.where(down, second, first)[None],
        jnp.where(down, first, third)[None],
    )


def solution(mesh):
    in_specs = (
        P(None, "dp", None),
        P(None, "dp", None),
        P(None, "dp"),
        P("segment", None, None),
        P("segment", None, None),
        P("segment", None, None),
        P("segment", None, None),
    )
    out_specs = (
        P("segment", None, "dp", None),
        P("segment", None, "dp", None),
        P("segment", "dp", None),
        P("segment", "dp", None),
        P("segment", "dp", None),
    )
    return jax.shard_map(body, mesh=mesh, in_specs=in_specs, out_specs=out_specs, check_vma=False)
```

```python
import functools
import types

import jax
import jax.numpy as jnp
from jax import lax
from jax.experimental import pallas as pl
from jax.experimental.pallas import tpu as pltpu
from jax.sharding import PartitionSpec as P

F32 = jnp.float32
BF16 = jnp.bfloat16
WITHIN = [(0, 1), (1, 0), (2, 3), (3, 2)]
UPWARD = [(0, 1), (1, 2), (2, 3), (3, 0)]
DOWNWARD = [(1, 0), (2, 1), (3, 2), (0, 3)]
DOWN, UP = (0, 1), (2, 3)
VMEM = pl.BlockSpec(memory_space=pltpu.VMEM)
HBM = pl.BlockSpec(memory_space=pltpu.HBM)
SMEM = pl.BlockSpec(memory_space=pltpu.SMEM)
ANY = pl.BlockSpec(memory_space=pl.ANY)
LANES = 128


def dot(a, b):
    return jnp.dot(a, b, preferred_element_type=F32)


def sigmoid(v):
    return 1.0 / (1.0 + jnp.exp(-v))


def silu_grad(pre):
    sig = sigmoid(pre)
    return sig * (1.0 + pre * (1.0 - sig))


def on_section(*slots):
    seg = lax.axis_index("segment")
    hit = seg == slots[0]
    for s in slots[1:]:
        hit = hit | (seg == s)
    return pl.when(hit)


class Chain:
    def __init__(self):
        self.stores = {}

    def call(self, kernel, args, outs, name, new=(), drop=(), specs=None, scratch=(), after=(), to_hbm=()):
        for key in drop:
            self.stores.pop(key)
        held = list(self.stores)
        made = dict(new)
        ins, extra = len(args), len(after)

        def run(*refs):
            here = refs[ins + extra + len(held) :]
            results, here = here[: len(outs)], here[len(outs) :]
            names = held + list(made)
            kernel(
                types.SimpleNamespace(**dict(zip(names, here))),
                *refs[:ins],
                *results,
                *here[len(names) :],
            )

        in_vmem = lambda a: pltpu.with_memory_space_constraint(a, pltpu.VMEM)
        specs = list(specs or [VMEM] * ins)
        values = [
            pltpu.with_memory_space_constraint(a, pltpu.HBM) if spec is HBM else a
            for a, spec in zip(args, specs)
        ]
        stores = [self.stores[key] for key in held]
        shapes = list(outs) + [(a.shape, a.dtype) for a in stores] + list(made.values())
        results = pl.pallas_call(
            run,
            out_shape=[
                (pltpu.HBM if k in to_hbm else pltpu.VMEM)(shape, dtype) for k, (shape, dtype) in enumerate(shapes)
            ],
            in_specs=specs + [ANY] * extra + [VMEM] * len(held),
            out_specs=[HBM if k in to_hbm else VMEM for k in range(len(shapes))],
            scratch_shapes=list(scratch),
            input_output_aliases={ins + extra + k: len(outs) + k for k in range(len(held))},
            name=name,
            compiler_params=pltpu.CompilerParams(vmem_limit_bytes=12 * 2**20),
            cost_estimate=pl.CostEstimate(flops=1000, bytes_accessed=1000, transcendentals=0),
        )(*values, *after, *[in_vmem(a) for a in stores])
        self.stores = dict(zip(held + list(made), results[len(outs) :]))
        return results[: len(outs)]


def pieces(source, target, sems, first, count=4):
    rows = target.shape[0] // count
    return [
        pltpu.make_async_copy(
            source.at[pl.ds(k * rows, rows)], target.at[pl.ds(k * rows, rows)], sems.at[first + k]
        )
        for k in range(count)
    ]


def place(m, rows):
    return pl.ds(m * rows, rows)


def finish_forward(s, at, x, pre):
    s.pre[at, :] = pre
    gated = (pre * sigmoid(pre)).astype(BF16)
    s.gated[at, :] = gated
    out = (x.astype(F32) + dot(gated, s.wo[...])).astype(BF16)
    s.out[at, :] = out
    return out


def start_kernel(micro, rows, s, steps_ref, x_hbm, cot_hbm, table_hbm, wi_hbm, wo_hbm, out_ref, table_ref, sems):
    load_x = [pltpu.make_async_copy(x_hbm.at[m], s.x.at[place(m, rows)], sems.at[m]) for m in range(micro)]
    load_cot = [
        pltpu.make_async_copy(cot_hbm.at[m], s.total.at[place(m, rows)], sems.at[micro + m]) for m in range(micro)
    ]
    load_table = [pltpu.make_async_copy(table_hbm.at[0], table_ref, sems.at[2 * micro])]
    load_wi = pieces(wi_hbm.at[0], s.wi, sems, 2 * micro + 1)
    load_wo = pieces(wo_hbm.at[0], s.wo, sems, 2 * micro + 5)
    for load in load_table + load_x + load_wi + load_wo + load_cot:
        load.start()
    count = table_ref.shape[0]
    row = lax.broadcasted_iota(jnp.int32, (s.bias.shape[0], count), 0)
    col = lax.broadcasted_iota(jnp.int32, (s.bias.shape[0], count), 1)
    wanted = jnp.full(row.shape, -1, jnp.int32)
    for m in range(micro):
        wanted = jnp.where(row == m, steps_ref[m, 0], wanted)
    chosen = (col == wanted).astype(F32).astype(BF16)
    for load in load_table:
        load.wait()
    s.bias[...] = dot(chosen, table_ref[...])
    for load in load_x + load_wi:
        load.wait()
    at = place(0, rows)

    @on_section(0)
    def _():
        s.pre[at, :] = dot(s.x[at, :], s.wi[...]) + s.bias[0:1, :]

    for load in load_wo:
        load.wait()

    @on_section(0)
    def _():
        out_ref[...] = finish_forward(s, at, s.x[at, :], s.pre[at, :])

    for load in load_cot:
        load.wait()


def first_skip_kernel(rows, s, ws_hbm, skip_ref, sems):
    loads = pieces(ws_hbm.at[0], s.ws, sems, 0)
    for load in loads:
        load.start()
    for load in loads:
        load.wait()

    @on_section(0)
    def _():
        skip_ref[...] = dot(s.out[place(0, rows), :], s.ws[...]).astype(BF16)


def skip_kernel(m, rows, s, skip_ref):
    @on_section(0)
    def _():
        skip_ref[...] = dot(s.out[place(m, rows), :], s.ws[...]).astype(BF16)


def forward0_kernel(m, rows, s, out_ref):
    @on_section(0)
    def _():
        at = place(m, rows)
        x = s.x[at, :]
        out_ref[...] = finish_forward(s, at, x, dot(x, s.wi[...]) + s.bias[m : m + 1, :])


def forward1_kernel(m, rows, s, x_ref, pair_ref):
    @on_section(1)
    def _():
        at = place(m, rows)
        x = x_ref[...]
        s.x[at, :] = x
        out = finish_forward(s, at, x, dot(x, s.wi[...]) + s.bias[m : m + 1, :])
        pair_ref[pl.ds(0, rows), :] = out
        pair_ref[pl.ds(rows, rows), :] = dot(out, s.ws[...]).astype(BF16)


def forward2_kernel(m, rows, s, pair_ref, out_ref):
    @on_section(2)
    def _():
        at = place(m, rows)
        x = pair_ref[pl.ds(0, rows), :]
        skip = pair_ref[pl.ds(rows, rows), :]
        s.x[at, :] = x
        s.side[at, :] = skip
        pre = dot(x, s.wi[...]) + dot(skip, s.ws[...]) + s.bias[m : m + 1, :]
        out_ref[...] = finish_forward(s, at, x, pre)


def add_skip_kernel(m, rows, s, skip_ref):
    @on_section(3)
    def _():
        at = place(m, rows)
        skip = skip_ref[...]
        s.side[at, :] = skip
        s.part[at, :] = dot(skip, s.ws[...]) + s.bias[m : m + 1, :]


def turn_kernel(slots, s):
    @on_section(*slots)
    def _():
        s.wo_t[...] = s.wo[...].T
        s.wi_t[...] = s.wi[...].T
        s.ws_t[...] = s.ws[...].T

    if 3 in slots:
        @on_section(3)
        def _():
            s.back[...] = dot(s.total[...], s.wo_t[...])


def turn3_kernel(m, rows, s, x_ref, d_in_ref):
    @on_section(3)
    def _():
        at = place(m, rows)
        x = x_ref[...]
        s.x[at, :] = x
        pre = s.part[at, :] + dot(x, s.wi[...])
        finish_forward(s, at, x, pre)
        d_pre = (s.back[at, :] * silu_grad(pre)).astype(BF16)
        s.d_pre[at, :] = d_pre
        d_in = (s.total[at, :].astype(F32) + dot(d_pre, s.wi_t[...])).astype(BF16)
        s.d_in[at, :] = d_in
        d_in_ref[...] = d_in


def dskip_kernel(m, rows, s, dskip_ref):
    @on_section(3)
    def _():
        dskip_ref[...] = dot(s.d_pre[place(m, rows), :], s.ws_t[...]).astype(BF16)


def finish_backward(s, at, total):
    s.total[at, :] = total
    d_pre = (dot(total, s.wo_t[...]) * silu_grad(s.pre[at, :])).astype(BF16)
    s.d_pre[at, :] = d_pre
    d_in = (total.astype(F32) + dot(d_pre, s.wi_t[...])).astype(BF16)
    s.d_in[at, :] = d_in
    return d_pre, d_in


def backward2_kernel(m, rows, s, total_ref, pair_ref):
    @on_section(2)
    def _():
        d_pre, d_in = finish_backward(s, place(m, rows), total_ref[...])
        pair_ref[pl.ds(0, rows), :] = d_in
        pair_ref[pl.ds(rows, rows), :] = dot(d_pre, s.ws_t[...]).astype(BF16)


def down_backward(m, rows, s, up):
    at = place(m, rows)
    total = (up.astype(F32) + dot(s.side[at, :], s.ws_t[...])).astype(BF16)
    return finish_backward(s, at, total)[1]


def backward1_kernel(m, rows, s, pair_ref, d_in_ref):
    @on_section(1)
    def _():
        s.side[place(m, rows), :] = pair_ref[pl.ds(rows, rows), :]
        d_in_ref[...] = down_backward(m, rows, s, pair_ref[pl.ds(0, rows), :])


def backward0_kernel(m, rows, s, up_ref):
    @on_section(0)
    def _():
        down_backward(m, rows, s, up_ref[...])


def block_order(steps):
    order = [0]
    for step in reversed(steps):
        order = [r | step for r in order] + order
    return order


def lefts_kernel(slots, devices, micro, rows, names, shared, steps, s, far_ref, turned, gathered):
    width = turned.shape[0]
    block, half = width // devices, width // 2
    dp_id = lax.axis_index("dp")

    @on_section(*slots)
    def _():
        for i, (store, name) in enumerate(names):
            for m in range(micro):
                turned[...] = getattr(s, name)[place(m, rows), :].astype(F32).T
                for far in (0, shared):
                    for p, mask in enumerate(block_order(steps)):
                        at = pl.multiple_of(jnp.bitwise_xor(dp_id, mask ^ far) * block, 8)
                        gathered[pl.ds(p * block, block), :] = turned[pl.ds(at, block), :]
                    if far:
                        for j in range(half // LANES):
                            far_ref[place(m, rows), pl.ds(i * half + j * LANES, LANES)] = gathered[
                                pl.ds(j * LANES, LANES), :
                            ].astype(BF16)
                    else:
                        s.near[store, :, place(m, rows)] = gathered[...].astype(BF16)


def right_kernel(m, rows, s, dskip_ref, packed):
    at = place(m, rows)

    @on_section(0)
    def _():
        s.side[at, :] = dskip_ref[...]
        packed[...] = dskip_ref[...]

    @on_section(1)
    def _():
        packed[...] = s.side[at, :]

    @on_section(2, 3)
    def _():
        packed[...] = s.total[at, :]


def pack_kernel(m, rows, down, up, s, packed):
    for slots, name in ((DOWN, down), (UP, up)):
        if name:
            @on_section(*slots)
            def _(name=name):
                packed[...] = getattr(s, name)[...] if m is None else getattr(s, name)[place(m, rows), :]


def turned_order(count):
    order = [0]
    step = 1
    while step < count:
        order = [p * 2 for p in order] + [p * 2 + 1 for p in order]
        step *= 2
    return order


def grad_kernel(parts, block, rows, micro, down, up, keeps, dumps, s, far_down, far_up, *refs):
    *refs, left_ref, right_ref, sum_ref, sems = refs
    targets = refs[len(refs) - len(dumps) :]
    refs = refs[: len(refs) - len(dumps)]
    fars, sends = refs[: -len(parts)], refs[-len(parts) :]
    copies = [
        pltpu.make_async_copy(getattr(s, name).at[place(m, rows)], target.at[0, m], sems.at[k * micro + m])
        for k, (name, target) in enumerate(zip(dumps, targets))
        for m in range(micro)
    ]
    for copy in copies:
        copy.start()
    n = micro * rows
    half = left_ref.shape[0]
    for slots, (i, column, name, first), far in ((DOWN, down, far_down), (UP, up, far_up)):
        @on_section(*slots)
        def _(i=i, column=column, name=name, first=first, far=far):
            left_ref[:, pl.ds(0, n)] = s.near[i]
            right_ref[pl.ds(0, n), :] = getattr(s, name)[...]
            at = n
            for k in range(first, first + micro):
                if at < 2 * n:
                    size = fars[k].shape[0]
                    right_ref[pl.ds(at, size), :] = fars[k][...]
                    at += size
            for m in range(micro):
                for j in range(half // LANES):
                    left_ref[pl.ds(j * LANES, LANES), pl.ds(n + m * rows, rows)] = far[
                        place(m, rows), pl.ds(column * half + j * LANES, LANES)
                    ]

    cut = half // 2
    for (start, size, turned), send_ref, keep in zip(parts, sends, keeps):
        keep_ref = getattr(s, keep)
        right = right_ref[:, pl.ds(start, size)]
        if not turned:
            send_ref[...] = dot(left_ref[pl.ds(0, cut), :], right).astype(BF16)
            keep_ref[...] = dot(left_ref[pl.ds(cut, cut), :], right)
        else:
            sum_ref[:, pl.ds(0, size)] = dot(left_ref[...], right)
            order = turned_order(half // block)
            picked = [sum_ref[pl.ds(p * block, block), pl.ds(0, size)] for p in order]
            middle = len(order) // 2
            send_ref[...] = jnp.concatenate(picked[:middle], axis=0).astype(BF16)
            keep_ref[...] = jnp.concatenate(picked[middle:], axis=0)
    for copy in copies:
        copy.wait()


def merge_kernel(keep, rest, s, far_ref, near_ref):
    cut = near_ref.shape[0]
    total = getattr(s, keep)[...] + far_ref[...].astype(F32)
    near_ref[...] = total[:cut].astype(BF16)
    getattr(s, rest)[...] = total[cut:]


def flip(x, bit, sections=None):
    devices = lax.axis_size("dp")
    if sections is None:
        return lax.ppermute(x, "dp", [(i, i ^ bit) for i in range(devices)])
    pairs = [(s * devices + i, s * devices + (i ^ bit)) for s in sections for i in range(devices)]
    return lax.ppermute(x, ("segment", "dp"), pairs)


def body(latents, cotangent, timesteps, time_table, w_in, w_out, w_skip):
    devices = lax.axis_size("dp")
    last = lax.axis_size("segment") - 1
    micro, rows, width = latents.shape
    ms = range(micro)
    n, half, block = micro * rows, width // 2, width // devices
    act, pair = ((rows, width), BF16), ((2 * rows, width), BF16)
    whole, weight = ((n, width), BF16), ((width, width), BF16)
    chain = Chain()
    send = lambda x, pairs: lax.ppermute(x, "segment", pairs)
    bound = functools.partial

    bits = [1 << k for k in range(devices.bit_length() - 1)]
    by_y, by_z = (bits[0], bits[1:]), (bits[1], bits[:1] + bits[2:])

    def lefts(slots, names, name, way, after=(), drop=(), tall=n):
        shared, steps = way
        far = chain.call(
            bound(lefts_kernel, slots, devices, micro, rows, names, shared, steps), [],
            [((tall, len(names) * half), BF16)], name,
            scratch=[pltpu.VMEM((width, rows), F32), pltpu.VMEM((half, rows), F32)], after=after, drop=drop)[0]
        return flip(far, shared, slots)

    def share(m, down, up, name, way, sections=None, after=()):
        shape = ((n if m is None else rows, width), BF16)
        packed = chain.call(bound(pack_kernel, m, rows, down, up), [], [shape], name, after=after)[0]
        return flip(packed, way[0], sections)

    def grad(parts, way, down, up, far_down, far_up, fars, name, dumps=(), after=()):
        keeps = [f"{name}_{k}" for k in range(len(parts))]
        sends = chain.call(
            bound(grad_kernel, parts, block, rows, micro, down, up, keeps, dumps), [far_down, far_up, *fars],
            [((half // 2, size), BF16) for _, size, _ in parts] + [((1, micro, rows, width), BF16)] * len(dumps), name,
            new=[(key, ((half // 2, size), F32)) for key, (_, size, _) in zip(keeps, parts)],
            scratch=[
                pltpu.VMEM((half, 2 * n), BF16), pltpu.VMEM((2 * n, width), BF16), pltpu.VMEM((half, width), F32),
                pltpu.SemaphoreType.DMA((2 * micro,)),
            ],
            to_hbm=[len(parts) + k for k in range(len(dumps))], after=after)
        states = []
        for (_, _, turned), key, out in zip(parts, keeps, sends):
            left = way[1][::-1] if turned else way[1]
            states.append((key, flip(out, left[0]), left[1:]))
        return (states, *sends[len(parts) :])

    def merge(state, after=()):
        key, far, steps = state
        if not steps:
            return state
        rest = key + "m"
        cut, size = far.shape[0] // 2, far.shape[1]
        near = chain.call(
            bound(merge_kernel, key, rest), [far], [((cut, size), BF16)], "merge",
            new=[(rest, ((cut, size), F32))], after=after)[0]
        chain.stores.pop(key)
        return rest, flip(near, steps[0]), steps[1:]

    names16 = ("x", "gated", "out", "side", "total", "d_pre", "d_in")
    stores = [(k, weight) for k in ("wi", "wo", "ws", "wi_t", "wo_t", "ws_t")]
    stores += [(k, whole) for k in names16] + [(k, ((n, width), F32)) for k in ("pre", "part", "back")]
    stores += [("bias", ((16, width), F32)), ("near", ((3, half, n), BF16))]
    x1, skip0, far1, x3, total2, dskip0, far2, up0 = ([None] * micro for _ in range(8))

    out = chain.call(
        bound(start_kernel, micro, rows), [timesteps, latents, cotangent, time_table, w_in, w_out], [act], "start",
        new=stores, specs=[SMEM, HBM, HBM, HBM, HBM, HBM],
        scratch=[pltpu.VMEM(time_table.shape[1:], BF16), pltpu.SemaphoreType.DMA((2 * micro + 9,))])[0]
    x1[0] = send(out, WITHIN)
    skip = chain.call(
        bound(first_skip_kernel, rows), [w_skip], [act], "skip0", specs=[HBM],
        scratch=[pltpu.SemaphoreType.DMA((4,))])[0]
    skip0[0] = send(skip, [(0, last)])
    for m in ms[1:]:
        x1[m] = send(chain.call(bound(forward0_kernel, m, rows), [], [act], "forward0")[0], WITHIN)
    for m in ms[1:]:
        skip0[m] = send(chain.call(bound(skip_kernel, m, rows), [], [act], "skip0")[0], [(0, last)])
    chain.call(bound(turn_kernel, UP), [], [], "turn_up")
    for m in ms:
        far1[m] = send(chain.call(bound(forward1_kernel, m, rows), [x1[m]], [pair], "forward1")[0], UPWARD)

    tall = n + (n // 2 + 16)
    down_z = lefts(DOWN, [(1, "gated")], "lefts_down", by_z, tall=2 * tall)
    down_y = lefts(DOWN, [(2, "out"), (0, "x")], "lefts_down", by_y, tall=tall)

    def forward2(m):
        chain.call(bound(add_skip_kernel, m, rows), [skip0[m]], [], "part3")
        x3[m] = send(chain.call(bound(forward2_kernel, m, rows), [far1[m]], [act], "forward2")[0], WITHIN)

    def turn3(m):
        total2[m] = send(chain.call(bound(turn3_kernel, m, rows), [x3[m]], [act], "turn3")[0], WITHIN)
        dskip0[m] = send(chain.call(bound(dskip_kernel, m, rows), [], [act], "dskip0")[0], [(last, 0)])

    def backward2(m):
        far2[m] = send(
            chain.call(bound(backward2_kernel, m, rows), [total2[m]], [pair], "backward2")[0], DOWNWARD)

    forward2(0)
    chain.call(bound(turn_kernel, DOWN), [], [], "turn_down")
    turn3(0)
    for m in ms[1:]:
        forward2(m)
        backward2(m - 1)
        turn3(m)
    backward2(micro - 1)
    up_y = lefts(UP, [(1, "gated")], "lefts_up", by_y, [dskip0[0], down_z, down_y], ("part", "back"))
    up_z = lefts(UP, [(0, "x")], "lefts_up", by_z)
    up_y2 = lefts(UP, [(2, "side")], "lefts_up", by_y)
    for key in ("x", "gated"):
        chain.stores.pop(key)
    rights1 = []
    for m in ms:
        up0[m] = send(
            chain.call(bound(backward1_kernel, m, rows), [far2[m]], [act], "backward1")[0],
            WITHIN)
        packed = chain.call(
            bound(right_kernel, m, rows), [dskip0[m]], [act], "right1", after=rights1 or [up_y])[0]
        rights1.append(flip(packed, by_y[0]))
        chain.call(
            bound(backward0_kernel, m, rows), [up0[m]], [], "backward0", after=[up_z] if m == micro - 1 else [])
    right2 = share(None, "total", "d_pre", "right2", by_z)
    right3 = share(None, "d_pre", "d_pre", "right3", by_y)
    for key in ("wi", "wo", "ws", "wi_t", "wo_t", "ws_t", "pre", "bias"):
        chain.stores.pop(key)

    cut = width // 2
    mixed = [(0, cut, False), (cut, width - cut, True)]
    plain = [(0, cut, False), (cut, width - cut, False)]
    (first,) = grad(
        mixed, by_y, (2, 0, "side", 0), (1, 0, "total", 0), down_y, up_y, rights1, "grad1")
    (second,) = grad(plain, by_z, (1, 0, "total", 0), (0, 0, "d_pre", 0), down_z, up_z, [right2], "grad2")
    third, phase_out, input_grads = grad(
        plain, by_y, (0, 1, "d_pre", 0), (2, 0, "d_pre", 0), down_y, up_y2, [right3], "grad3", ("out", "d_in"))
    for key in ("side", "total", "d_pre", "near", "out", "d_in"):
        chain.stores.pop(key)
    states = first[::-1] + second + third
    while states[0][2]:
        done = []
        for k, state in enumerate(states):
            after = [s[1] for s in done[k - 3 : k - 1]] if k in (3, 5) else []
            done.append(merge(state, after))
        states = done
    states = states[1::-1] + states[2:]
    sums = [chain.stores[key] + far.astype(F32) for key, far, _ in states]
    first, second, third = (jnp.concatenate(sums[k : k + 2], axis=1) for k in (0, 2, 4))
    down = lax.axis_index("segment") < 2
    return (
        phase_out,
        input_grads,
        jnp.where(down, third, second)[None],
        jnp.where(down, second, first)[None],
        jnp.where(down, first, third)[None],
    )


def solution(mesh):
    in_specs = (
        P(None, "dp", None),
        P(None, "dp", None),
        P(None, "dp"),
        P("segment", None, None),
        P("segment", None, None),
        P("segment", None, None),
        P("segment", None, None),
    )
    out_specs = (
        P("segment", None, "dp", None),
        P("segment", None, "dp", None),
        P("segment", "dp", None),
        P("segment", "dp", None),
        P("segment", "dp", None),
    )
    return jax.shard_map(body, mesh=mesh, in_specs=in_specs, out_specs=out_specs, check_vma=False)
```

```python
import functools
import types

import jax
import jax.numpy as jnp
from jax import lax
from jax.experimental import pallas as pl
from jax.experimental.pallas import tpu as pltpu
from jax.sharding import PartitionSpec as P

F32 = jnp.float32
BF16 = jnp.bfloat16
WITHIN = [(0, 1), (1, 0), (2, 3), (3, 2)]
UPWARD = [(0, 1), (1, 2), (2, 3), (3, 0)]
DOWNWARD = [(1, 0), (2, 1), (3, 2), (0, 3)]
DOWN, UP = (0, 1), (2, 3)
VMEM = pl.BlockSpec(memory_space=pltpu.VMEM)
HBM = pl.BlockSpec(memory_space=pltpu.HBM)
SMEM = pl.BlockSpec(memory_space=pltpu.SMEM)
ANY = pl.BlockSpec(memory_space=pl.ANY)
LANES = 128


def dot(a, b):
    return jnp.dot(a, b, preferred_element_type=F32)


def sigmoid(v):
    return 1.0 / (1.0 + jnp.exp(-v))


def silu_grad(pre):
    sig = sigmoid(pre)
    return sig * (1.0 + pre * (1.0 - sig))


def on_section(*slots):
    seg = lax.axis_index("segment")
    hit = seg == slots[0]
    for s in slots[1:]:
        hit = hit | (seg == s)
    return pl.when(hit)


class Chain:
    def __init__(self):
        self.stores = {}

    def call(self, kernel, args, outs, name, new=(), drop=(), specs=None, scratch=(), after=(), to_hbm=()):
        for key in drop:
            self.stores.pop(key)
        held = list(self.stores)
        made = dict(new)
        ins, extra = len(args), len(after)

        def run(*refs):
            here = refs[ins + extra + len(held) :]
            results, here = here[: len(outs)], here[len(outs) :]
            names = held + list(made)
            kernel(
                types.SimpleNamespace(**dict(zip(names, here))),
                *refs[:ins],
                *results,
                *here[len(names) :],
            )

        in_vmem = lambda a: pltpu.with_memory_space_constraint(a, pltpu.VMEM)
        specs = list(specs or [VMEM] * ins)
        values = [
            pltpu.with_memory_space_constraint(a, pltpu.HBM) if spec is HBM else a
            for a, spec in zip(args, specs)
        ]
        stores = [self.stores[key] for key in held]
        shapes = list(outs) + [(a.shape, a.dtype) for a in stores] + list(made.values())
        results = pl.pallas_call(
            run,
            out_shape=[
                (pltpu.HBM if k in to_hbm else pltpu.VMEM)(shape, dtype) for k, (shape, dtype) in enumerate(shapes)
            ],
            in_specs=specs + [ANY] * extra + [VMEM] * len(held),
            out_specs=[HBM if k in to_hbm else VMEM for k in range(len(shapes))],
            scratch_shapes=list(scratch),
            input_output_aliases={ins + extra + k: len(outs) + k for k in range(len(held))},
            name=name,
            compiler_params=pltpu.CompilerParams(vmem_limit_bytes=12 * 2**20),
            cost_estimate=pl.CostEstimate(flops=1000, bytes_accessed=1000, transcendentals=0),
        )(*values, *after, *[in_vmem(a) for a in stores])
        self.stores = dict(zip(held + list(made), results[len(outs) :]))
        return results[: len(outs)]


def pieces(source, target, sems, first, count=4):
    rows = target.shape[0] // count
    return [
        pltpu.make_async_copy(
            source.at[pl.ds(k * rows, rows)], target.at[pl.ds(k * rows, rows)], sems.at[first + k]
        )
        for k in range(count)
    ]


def place(m, rows):
    return pl.ds(m * rows, rows)


def finish_forward(s, at, x, pre):
    s.pre[at, :] = pre
    gated = (pre * sigmoid(pre)).astype(BF16)
    s.gated[at, :] = gated
    out = (x.astype(F32) + dot(gated, s.wo[...])).astype(BF16)
    s.out[at, :] = out
    return out


def start_kernel(micro, rows, s, steps_ref, x_hbm, table_hbm, wi_hbm, wo_hbm, out_ref, table_ref, sems):
    load_x = [pltpu.make_async_copy(x_hbm.at[m], s.x.at[place(m, rows)], sems.at[m]) for m in range(micro)]
    load_table = [pltpu.make_async_copy(table_hbm.at[0], table_ref, sems.at[2 * micro])]
    load_wi = pieces(wi_hbm.at[0], s.wi, sems, 2 * micro + 1)
    load_wo = pieces(wo_hbm.at[0], s.wo, sems, 2 * micro + 5)
    for load in load_table + load_x + load_wi + load_wo:
        load.start()
    count = table_ref.shape[0]
    row = lax.broadcasted_iota(jnp.int32, (s.bias.shape[0], count), 0)
    col = lax.broadcasted_iota(jnp.int32, (s.bias.shape[0], count), 1)
    wanted = jnp.full(row.shape, -1, jnp.int32)
    for m in range(micro):
        wanted = jnp.where(row == m, steps_ref[m, 0], wanted)
    chosen = (col == wanted).astype(F32).astype(BF16)
    for load in load_table:
        load.wait()
    s.bias[...] = dot(chosen, table_ref[...])
    for load in load_x + load_wi:
        load.wait()
    at = place(0, rows)

    @on_section(0)
    def _():
        s.pre[at, :] = dot(s.x[at, :], s.wi[...]) + s.bias[0:1, :]

    for load in load_wo:
        load.wait()

    @on_section(0)
    def _():
        out_ref[...] = finish_forward(s, at, s.x[at, :], s.pre[at, :])


def first_skip_kernel(micro, rows, s, ws_hbm, cot_hbm, skip_ref, sems):
    loads = pieces(ws_hbm.at[0], s.ws, sems, 0)
    loads += [
        pltpu.make_async_copy(cot_hbm.at[m], s.total.at[place(m, rows)], sems.at[4 + m]) for m in range(micro)
    ]
    for load in loads:
        load.start()
    for load in loads:
        load.wait()

    @on_section(0)
    def _():
        skip_ref[...] = dot(s.out[place(0, rows), :], s.ws[...]).astype(BF16)


def skip_kernel(m, rows, s, skip_ref):
    @on_section(0)
    def _():
        skip_ref[...] = dot(s.out[place(m, rows), :], s.ws[...]).astype(BF16)


def forward0_kernel(m, rows, s, out_ref):
    @on_section(0)
    def _():
        at = place(m, rows)
        x = s.x[at, :]
        out_ref[...] = finish_forward(s, at, x, dot(x, s.wi[...]) + s.bias[m : m + 1, :])


def forward1_kernel(m, rows, s, x_ref, pair_ref):
    @on_section(1)
    def _():
        at = place(m, rows)
        x = x_ref[...]
        s.x[at, :] = x
        out = finish_forward(s, at, x, dot(x, s.wi[...]) + s.bias[m : m + 1, :])
        pair_ref[pl.ds(0, rows), :] = out
        pair_ref[pl.ds(rows, rows), :] = dot(out, s.ws[...]).astype(BF16)


def forward2_kernel(m, rows, s, pair_ref, out_ref):
    @on_section(2)
    def _():
        at = place(m, rows)
        x = pair_ref[pl.ds(0, rows), :]
        skip = pair_ref[pl.ds(rows, rows), :]
        s.x[at, :] = x
        s.side[at, :] = skip
        pre = dot(x, s.wi[...]) + dot(skip, s.ws[...]) + s.bias[m : m + 1, :]
        out_ref[...] = finish_forward(s, at, x, pre)


def add_skip_kernel(m, rows, s, skip_ref):
    @on_section(3)
    def _():
        at = place(m, rows)
        skip = skip_ref[...]
        s.side[at, :] = skip
        s.part[at, :] = dot(skip, s.ws[...]) + s.bias[m : m + 1, :]


def turn_kernel(slots, s):
    @on_section(*slots)
    def _():
        s.wo_t[...] = s.wo[...].T
        s.wi_t[...] = s.wi[...].T
        s.ws_t[...] = s.ws[...].T

    if 3 in slots:
        @on_section(3)
        def _():
            s.back[...] = dot(s.total[...], s.wo_t[...])


def turn3_kernel(m, rows, s, x_ref, d_in_ref):
    @on_section(3)
    def _():
        at = place(m, rows)
        x = x_ref[...]
        s.x[at, :] = x
        pre = s.part[at, :] + dot(x, s.wi[...])
        finish_forward(s, at, x, pre)
        d_pre = (s.back[at, :] * silu_grad(pre)).astype(BF16)
        s.d_pre[at, :] = d_pre
        d_in = (s.total[at, :].astype(F32) + dot(d_pre, s.wi_t[...])).astype(BF16)
        s.d_in[at, :] = d_in
        d_in_ref[...] = d_in


def dskip_kernel(m, rows, s, dskip_ref):
    @on_section(3)
    def _():
        dskip_ref[...] = dot(s.d_pre[place(m, rows), :], s.ws_t[...]).astype(BF16)


def finish_backward(s, at, total):
    s.total[at, :] = total
    d_pre = (dot(total, s.wo_t[...]) * silu_grad(s.pre[at, :])).astype(BF16)
    s.d_pre[at, :] = d_pre
    d_in = (total.astype(F32) + dot(d_pre, s.wi_t[...])).astype(BF16)
    s.d_in[at, :] = d_in
    return d_pre, d_in


def backward2_kernel(m, rows, s, total_ref, pair_ref):
    @on_section(2)
    def _():
        d_pre, d_in = finish_backward(s, place(m, rows), total_ref[...])
        pair_ref[pl.ds(0, rows), :] = d_in
        pair_ref[pl.ds(rows, rows), :] = dot(d_pre, s.ws_t[...]).astype(BF16)


def down_backward(m, rows, s, up):
    at = place(m, rows)
    total = (up.astype(F32) + dot(s.side[at, :], s.ws_t[...])).astype(BF16)
    return finish_backward(s, at, total)[1]


def backward1_kernel(m, rows, s, pair_ref, d_in_ref):
    @on_section(1)
    def _():
        s.side[place(m, rows), :] = pair_ref[pl.ds(rows, rows), :]
        d_in_ref[...] = down_backward(m, rows, s, pair_ref[pl.ds(0, rows), :])


def backward0_kernel(m, rows, s, up_ref):
    @on_section(0)
    def _():
        down_backward(m, rows, s, up_ref[...])


def block_order(steps):
    order = [0]
    for step in reversed(steps):
        order = [r | step for r in order] + order
    return order


def lefts_kernel(slots, devices, micro, rows, names, shared, steps, s, far_ref, turned, gathered):
    width = turned.shape[0]
    block, half = width // devices, width // 2
    dp_id = lax.axis_index("dp")

    @on_section(*slots)
    def _():
        for i, (store, name) in enumerate(names):
            for m in range(micro):
                turned[...] = getattr(s, name)[place(m, rows), :].astype(F32).T
                for far in (0, shared):
                    for p, mask in enumerate(block_order(steps)):
                        at = pl.multiple_of(jnp.bitwise_xor(dp_id, mask ^ far) * block, 8)
                        gathered[pl.ds(p * block, block), :] = turned[pl.ds(at, block), :]
                    if far:
                        for j in range(half // LANES):
                            far_ref[place(m, rows), pl.ds(i * half + j * LANES, LANES)] = gathered[
                                pl.ds(j * LANES, LANES), :
                            ].astype(BF16)
                    else:
                        s.near[store, :, place(m, rows)] = gathered[...].astype(BF16)


def right_kernel(m, rows, s, dskip_ref, packed):
    at = place(m, rows)

    @on_section(0)
    def _():
        s.side[at, :] = dskip_ref[...]
        packed[...] = dskip_ref[...]

    @on_section(1)
    def _():
        packed[...] = s.side[at, :]

    @on_section(2, 3)
    def _():
        packed[...] = s.total[at, :]


def pack_kernel(m, rows, down, up, s, packed):
    for slots, name in ((DOWN, down), (UP, up)):
        if name:
            @on_section(*slots)
            def _(name=name):
                packed[...] = getattr(s, name)[...] if m is None else getattr(s, name)[place(m, rows), :]


def turned_order(count):
    order = [0]
    step = 1
    while step < count:
        order = [p * 2 for p in order] + [p * 2 + 1 for p in order]
        step *= 2
    return order


def grad_kernel(parts, block, rows, micro, down, up, keeps, dumps, s, far_down, far_up, *refs):
    *refs, left_ref, right_ref, sum_ref, sems = refs
    targets = refs[len(refs) - len(dumps) :]
    refs = refs[: len(refs) - len(dumps)]
    fars, sends = refs[: -len(parts)], refs[-len(parts) :]
    copies = [
        pltpu.make_async_copy(getattr(s, name).at[place(m, rows)], target.at[0, m], sems.at[k * micro + m])
        for k, (name, target) in enumerate(zip(dumps, targets))
        for m in range(micro)
    ]
    for copy in copies:
        copy.start()
    n = micro * rows
    half = left_ref.shape[0]
    for slots, (i, column, name, first), far in ((DOWN, down, far_down), (UP, up, far_up)):
        @on_section(*slots)
        def _(i=i, column=column, name=name, first=first, far=far):
            left_ref[:, pl.ds(0, n)] = s.near[i]
            right_ref[pl.ds(0, n), :] = getattr(s, name)[...]
            at = n
            for k in range(first, first + micro):
                if at < 2 * n:
                    size = fars[k].shape[0]
                    right_ref[pl.ds(at, size), :] = fars[k][...]
                    at += size
            for m in range(micro):
                for j in range(half // LANES):
                    left_ref[pl.ds(j * LANES, LANES), pl.ds(n + m * rows, rows)] = far[
                        place(m, rows), pl.ds(column * half + j * LANES, LANES)
                    ]

    cut = half // 2
    for (start, size, turned), send_ref, keep in zip(parts, sends, keeps):
        keep_ref = getattr(s, keep)
        right = right_ref[:, pl.ds(start, size)]
        if not turned:
            send_ref[...] = dot(left_ref[pl.ds(0, cut), :], right).astype(BF16)
            keep_ref[...] = dot(left_ref[pl.ds(cut, cut), :], right)
        else:
            sum_ref[:, pl.ds(0, size)] = dot(left_ref[...], right)
            order = turned_order(half // block)
            picked = [sum_ref[pl.ds(p * block, block), pl.ds(0, size)] for p in order]
            middle = len(order) // 2
            send_ref[...] = jnp.concatenate(picked[:middle], axis=0).astype(BF16)
            keep_ref[...] = jnp.concatenate(picked[middle:], axis=0)
    for copy in copies:
        copy.wait()


def merge_kernel(keep, rest, s, far_ref, near_ref):
    cut = near_ref.shape[0]
    total = getattr(s, keep)[...] + far_ref[...].astype(F32)
    near_ref[...] = total[:cut].astype(BF16)
    getattr(s, rest)[...] = total[cut:]


def flip(x, bit, sections=None):
    devices = lax.axis_size("dp")
    if sections is None:
        return lax.ppermute(x, "dp", [(i, i ^ bit) for i in range(devices)])
    pairs = [(s * devices + i, s * devices + (i ^ bit)) for s in sections for i in range(devices)]
    return lax.ppermute(x, ("segment", "dp"), pairs)


def body(latents, cotangent, timesteps, time_table, w_in, w_out, w_skip):
    devices = lax.axis_size("dp")
    last = lax.axis_size("segment") - 1
    micro, rows, width = latents.shape
    ms = range(micro)
    n, half, block = micro * rows, width // 2, width // devices
    act, pair = ((rows, width), BF16), ((2 * rows, width), BF16)
    whole, weight = ((n, width), BF16), ((width, width), BF16)
    chain = Chain()
    send = lambda x, pairs: lax.ppermute(x, "segment", pairs)
    bound = functools.partial

    bits = [1 << k for k in range(devices.bit_length() - 1)]
    by_y, by_z = (bits[0], bits[1:]), (bits[1], bits[:1] + bits[2:])

    def lefts(slots, names, name, way, after=(), drop=(), tall=n):
        shared, steps = way
        far = chain.call(
            bound(lefts_kernel, slots, devices, micro, rows, names, shared, steps), [],
            [((tall, len(names) * half), BF16)], name,
            scratch=[pltpu.VMEM((width, rows), F32), pltpu.VMEM((half, rows), F32)], after=after, drop=drop)[0]
        return flip(far, shared, slots)

    def share(m, down, up, name, way, sections=None, after=()):
        shape = ((n if m is None else rows, width), BF16)
        packed = chain.call(bound(pack_kernel, m, rows, down, up), [], [shape], name, after=after)[0]
        return flip(packed, way[0], sections)

    def grad(parts, way, down, up, far_down, far_up, fars, name, dumps=(), after=()):
        keeps = [f"{name}_{k}" for k in range(len(parts))]
        sends = chain.call(
            bound(grad_kernel, parts, block, rows, micro, down, up, keeps, dumps), [far_down, far_up, *fars],
            [((half // 2, size), BF16) for _, size, _ in parts] + [((1, micro, rows, width), BF16)] * len(dumps), name,
            new=[(key, ((half // 2, size), F32)) for key, (_, size, _) in zip(keeps, parts)],
            scratch=[
                pltpu.VMEM((half, 2 * n), BF16), pltpu.VMEM((2 * n, width), BF16), pltpu.VMEM((half, width), F32),
                pltpu.SemaphoreType.DMA((2 * micro,)),
            ],
            to_hbm=[len(parts) + k for k in range(len(dumps))], after=after)
        states = []
        for (_, _, turned), key, out in zip(parts, keeps, sends):
            left = way[1][::-1] if turned else way[1]
            states.append((key, flip(out, left[0]), left[1:]))
        return (states, *sends[len(parts) :])

    def merge(state, after=()):
        key, far, steps = state
        if not steps:
            return state
        rest = key + "m"
        cut, size = far.shape[0] // 2, far.shape[1]
        near = chain.call(
            bound(merge_kernel, key, rest), [far], [((cut, size), BF16)], "merge",
            new=[(rest, ((cut, size), F32))], after=after)[0]
        chain.stores.pop(key)
        return rest, flip(near, steps[0]), steps[1:]

    names16 = ("x", "gated", "out", "side", "total", "d_pre", "d_in")
    stores = [(k, weight) for k in ("wi", "wo", "ws", "wi_t", "wo_t", "ws_t")]
    stores += [(k, whole) for k in names16] + [(k, ((n, width), F32)) for k in ("pre", "part", "back")]
    stores += [("bias", ((16, width), F32)), ("near", ((3, half, n), BF16))]
    x1, skip0, far1, x3, total2, dskip0, far2, up0 = ([None] * micro for _ in range(8))

    out = chain.call(
        bound(start_kernel, micro, rows), [timesteps, latents, time_table, w_in, w_out], [act], "start",
        new=stores, specs=[SMEM, HBM, HBM, HBM, HBM],
        scratch=[pltpu.VMEM(time_table.shape[1:], BF16), pltpu.SemaphoreType.DMA((2 * micro + 9,))])[0]
    x1[0] = send(out, WITHIN)
    skip = chain.call(
        bound(first_skip_kernel, micro, rows), [w_skip, cotangent], [act], "skip0", specs=[HBM, HBM],
        scratch=[pltpu.SemaphoreType.DMA((4 + micro,))])[0]
    skip0[0] = send(skip, [(0, last)])
    for m in ms[1:]:
        x1[m] = send(chain.call(bound(forward0_kernel, m, rows), [], [act], "forward0")[0], WITHIN)
    for m in ms[1:]:
        skip0[m] = send(chain.call(bound(skip_kernel, m, rows), [], [act], "skip0")[0], [(0, last)])
    chain.call(bound(turn_kernel, UP), [], [], "turn_up")
    for m in ms:
        far1[m] = send(chain.call(bound(forward1_kernel, m, rows), [x1[m]], [pair], "forward1")[0], UPWARD)

    tall = n + (n // 2 + 16)
    down_z = lefts(DOWN, [(1, "gated")], "lefts_down", by_z, tall=2 * tall)
    down_y = lefts(DOWN, [(2, "out"), (0, "x")], "lefts_down", by_y, tall=tall)

    def forward2(m):
        chain.call(bound(add_skip_kernel, m, rows), [skip0[m]], [], "part3")
        x3[m] = send(chain.call(bound(forward2_kernel, m, rows), [far1[m]], [act], "forward2")[0], WITHIN)

    def turn3(m):
        total2[m] = send(chain.call(bound(turn3_kernel, m, rows), [x3[m]], [act], "turn3")[0], WITHIN)
        dskip0[m] = send(chain.call(bound(dskip_kernel, m, rows), [], [act], "dskip0")[0], [(last, 0)])

    def backward2(m):
        far2[m] = send(
            chain.call(bound(backward2_kernel, m, rows), [total2[m]], [pair], "backward2")[0], DOWNWARD)

    forward2(0)
    chain.call(bound(turn_kernel, DOWN), [], [], "turn_down")
    turn3(0)
    for m in ms[1:]:
        forward2(m)
        backward2(m - 1)
        turn3(m)
    backward2(micro - 1)
    up_y = lefts(UP, [(1, "gated")], "lefts_up", by_y, [dskip0[0], down_z, down_y], ("part", "back"))
    up_z = lefts(UP, [(0, "x")], "lefts_up", by_z)
    up_y2 = lefts(UP, [(2, "side")], "lefts_up", by_y)
    for key in ("x", "gated"):
        chain.stores.pop(key)
    rights1 = []
    for m in ms:
        up0[m] = send(
            chain.call(bound(backward1_kernel, m, rows), [far2[m]], [act], "backward1")[0],
            WITHIN)
        packed = chain.call(
            bound(right_kernel, m, rows), [dskip0[m]], [act], "right1", after=rights1 or [up_y])[0]
        rights1.append(flip(packed, by_y[0]))
        chain.call(
            bound(backward0_kernel, m, rows), [up0[m]], [], "backward0", after=[up_z] if m == micro - 1 else [])
    right2 = share(None, "total", "d_pre", "right2", by_z)
    right3 = share(None, "d_pre", "d_pre", "right3", by_y)
    for key in ("wi", "wo", "ws", "wi_t", "wo_t", "ws_t", "pre", "bias"):
        chain.stores.pop(key)

    cut = width // 2
    mixed = [(0, cut, False), (cut, width - cut, True)]
    plain = [(0, cut, False), (cut, width - cut, False)]
    (first,) = grad(
        mixed, by_y, (2, 0, "side", 0), (1, 0, "total", 0), down_y, up_y, rights1, "grad1")
    (second,) = grad(plain, by_z, (1, 0, "total", 0), (0, 0, "d_pre", 0), down_z, up_z, [right2], "grad2")
    third, phase_out, input_grads = grad(
        plain, by_y, (0, 1, "d_pre", 0), (2, 0, "d_pre", 0), down_y, up_y2, [right3], "grad3", ("out", "d_in"))
    for key in ("side", "total", "d_pre", "near", "out", "d_in"):
        chain.stores.pop(key)
    states = first[::-1] + second + third
    while states[0][2]:
        done = []
        for k, state in enumerate(states):
            after = [s[1] for s in done[k - 3 : k - 1]] if k in (3, 5) else []
            done.append(merge(state, after))
        states = done
    states = states[1::-1] + states[2:]
    sums = [chain.stores[key] + far.astype(F32) for key, far, _ in states]
    first, second, third = (jnp.concatenate(sums[k : k + 2], axis=1) for k in (0, 2, 4))
    down = lax.axis_index("segment") < 2
    return (
        phase_out,
        input_grads,
        jnp.where(down, third, second)[None],
        jnp.where(down, second, first)[None],
        jnp.where(down, first, third)[None],
    )


def solution(mesh):
    in_specs = (
        P(None, "dp", None),
        P(None, "dp", None),
        P(None, "dp"),
        P("segment", None, None),
        P("segment", None, None),
        P("segment", None, None),
        P("segment", None, None),
    )
    out_specs = (
        P("segment", None, "dp", None),
        P("segment", None, "dp", None),
        P("segment", "dp", None),
        P("segment", "dp", None),
        P("segment", "dp", None),
    )
    return jax.shard_map(body, mesh=mesh, in_specs=in_specs, out_specs=out_specs, check_vma=False)
```
